256 devices in a mesh: seq: 64 (over x, y_lo, z), rep: 4 (over y_hi, core).
Axes of the slice: x: 4, y: 4 (y_hi: 2, y_lo: 2; y = y_hi * 2 + y_lo), z: 8, core: 2. Of those that a mesh axis runs over, the one named last changes fastest.
Arguments:
- queries: bfloat16 [4, 16384, 384], P('rep', 'seq'), may hold values from -3 to 3
- keys: bfloat16 [4, 16384, 384], P('rep', 'seq'), may hold values from -9 to 9
- values: bfloat16 [4, 16384, 384], P('rep', 'seq'), may hold values from -6 to 6
- outputs: bfloat16 [4, 16384, 384], P('rep', 'seq'), may hold values from -6 to 6
- out_grad: bfloat16 [4, 16384, 768], P('rep', 'seq'), may hold values from -6 to 6
- out_weight: bfloat16 [384, 768], replicated, may hold values from -0.21875 to 0.21875
- slide_table: int32 [4, 128], P('rep'), may hold values from 0 to 63, never falling along the last dimension, each value on 1 to 4 neighbouring positions
Outputs:
- query_grad: bfloat16 [4, 16384, 384], P('rep', 'seq')
- key_grad: bfloat16 [4, 16384, 384], P('rep', 'seq')
- value_grad: bfloat16 [4, 16384, 384], P('rep', 'seq')
- weight_grad: float32 [384, 768], replicated
The draws below stay inside these ranges and needn't reach their ends.
Inputs may be any that keep to these rules, and one draw needn't show every extreme that they name: `slide_table`: in each replica the slide numbers never fall along the units, every slide of 0 to 63 holds 1 to 4 units, and some slide holds exactly 4 units.
All inputs are finite; a program needn't handle non-finite values.
Results may differ from the reference program's by a relative error of at most 0.012.
Values may be sent and summed in bfloat16 or wider, within the bound.
A program may use at most 64 MiB of HBM per device.

```python
import math
import jax
import jax.numpy as jnp
import numpy as np
from jax import lax

D = 768
HEADS = 6
HEAD = 64
FEATS = 384
TOK_DEV = 256
BLOCK = 128
TOKENS = 16384
NBLK = 128
MOST = 4
SLIDES = 64
N_REP = 4


def draw_keys(key, part):
    key = jax.random.fold_in(key, 11)
    first_key, second_key = jax.random.split(key)
    shape = (N_REP, TOKENS, HEADS * HEAD)
    base_values = jnp.clip(jax.random.normal(first_key, shape, jnp.float32), -3.0, 3.0)
    row_scale = jnp.exp(jax.random.uniform(second_key, (N_REP, TOKENS, 1), jnp.float32, math.log(0.3), math.log(3.0)))
    return (base_values * row_scale).astype(jnp.bfloat16)


def shard_levels(own_key, extent, cuts, low, largest):
    factor_of = 1.0
    for position, parts in cuts:
        steps = jax.random.uniform(jax.random.fold_in(jax.random.fold_in(own_key, 6), position), (parts,), jnp.float32, low / len(cuts), largest / len(cuts))
        factor_of = factor_of * jnp.repeat(jnp.exp(steps), extent[position] // parts).reshape((-1,) + (1,) * (len(extent) - 1 - position))
    return factor_of


def split_up(amount, total, bound, skew):
    weights = [(1 << 20) // math.isqrt(standing ** skew) + 1 for standing in range(2, amount + 1)]
    spare, holding = total - bound - (amount - 1), [1] * (amount - 1)
    while spare > 0:
        free = [i for i in range(amount - 1) if holding[i] < bound]
        pool, remaining = sum([weights[i] for i in free]), spare
        for i in free:
            more = min(bound - holding[i], max(1, remaining * weights[i] // pool), spare)
            holding[i] = holding[i] + more
            spare = spare - more
    return np.array([bound] + holding)


def uneven(key, number_of, total, most, slope):
    if number_of == 2:
        one = jax.random.randint(key, (), max(1, total - most), min(most, total - 1) + 1)
        return jnp.stack([one, total - one])
    tallies = jnp.asarray(split_up(number_of, total, most, slope), jnp.int32)
    pairs = (number_of - 1) // 2
    donor, sink = tallies[1:1 + 2 * pairs:2], tallies[2:2 + 2 * pairs:2]
    room = jnp.minimum(donor - 1, most - sink)
    moved = jax.random.randint(jax.random.fold_in(key, 1), (pairs,), 0, 1 << 20) % (room + 1)
    tallies = tallies.at[1:1 + 2 * pairs:2].set(donor - moved).at[2:2 + 2 * pairs:2].set(sink + moved)
    return tallies[jax.random.permutation(jax.random.fold_in(key, 2), number_of)]


def noise(own_key, dims, scale, most, cuts=(), kind=jnp.bfloat16):
    factor_of = shard_levels(own_key, dims, cuts, -0.22, 0.18) if cuts else 1.0
    result = jax.random.normal(own_key, dims, jnp.float32) * scale * factor_of
    return jnp.minimum(jnp.maximum(result, -most), most).astype(kind)


def setup_inputs(seed: int = 0) -> dict:
    arg_keys = jax.random.split(jax.random.key(seed), 8)
    return {
        "queries": noise(arg_keys[0], (N_REP, TOKENS, FEATS), 1.0, 3.0, ((0, 4), (1, 64))),
        "keys": draw_keys(jax.random.fold_in(arg_keys[7], 71), 0),
        "values": noise(arg_keys[2], (N_REP, TOKENS, FEATS), 1.0, 6.0, ((0, 4), (1, 64))),
        "outputs": noise(arg_keys[3], (N_REP, TOKENS, FEATS), 1.0, 6.0, ((0, 4), (1, 64))),
        "out_grad": noise(arg_keys[4], (N_REP, TOKENS, D), 1.0, 6.0, ((0, 4), (1, 64))),
        "out_weight": noise(arg_keys[5], (FEATS, D), D ** -0.5, 0.21875),
        "slide_table": jax.vmap(lambda own: jnp.searchsorted(jnp.cumsum(uneven(own, SLIDES, NBLK, MOST, 2)), jnp.arange(NBLK), side="right"))(jax.random.split(arg_keys[6], N_REP)).reshape((N_REP, NBLK)).astype(jnp.int32),
    }


def round_trip(values_in):
    rounded = values_in.astype(jnp.bfloat16)
    rounded = lax.optimization_barrier(rounded)
    return rounded.astype(jnp.float32)

def window_bounds(index):
    reach_rows = MOST * BLOCK
    window = min(TOKENS, TOK_DEV + 2 * reach_rows)
    start = (index * TOK_DEV).astype(jnp.int32)
    lower = jnp.clip(start - reach_rows, 0, TOKENS - window).astype(jnp.int32)
    return (start, lower, window)

def query_pass(q_heads, k_heads, v_heads, d_heads, deltas, token_ids):
    att_scale = 1.0 / math.sqrt(HEAD)

    def one_block(index):
        start, lower, window = window_bounds(index)
        q_part = lax.dynamic_slice_in_dim(q_heads, start, TOK_DEV, 0)
        d_part = lax.dynamic_slice_in_dim(d_heads, start, TOK_DEV, 0)
        delta_part = lax.dynamic_slice_in_dim(deltas, start, TOK_DEV, 0)
        ids_part = lax.dynamic_slice_in_dim(token_ids, start, TOK_DEV, 0)
        k_win = lax.dynamic_slice_in_dim(k_heads, lower, window, 0)
        v_win = lax.dynamic_slice_in_dim(v_heads, lower, window, 0)
        ids_win = lax.dynamic_slice_in_dim(token_ids, lower, window, 0)
        linked = ids_part[:, None] == ids_win[None, :]
        scores = jnp.einsum('qhd,khd->hqk', q_part, k_win) * att_scale
        expo = jnp.where(linked[None], jnp.exp(scores), 0.0)
        totals = lax.optimization_barrier(jnp.sum(expo, axis=2))
        d_prob = jnp.einsum('qhd,khd->hqk', d_part, v_win)
        weighted = round_trip(expo * (d_prob - delta_part.T[:, :, None]))
        numer = jnp.einsum('hqk,khd->qhd', weighted, k_win)
        grad = (att_scale * numer / totals.T[:, :, None]).astype(jnp.bfloat16)
        return (grad, totals.T)
    grads, totals = lax.map(one_block, jnp.arange(TOKENS // TOK_DEV, dtype=jnp.int32))
    return (grads.reshape(TOKENS, FEATS), totals.reshape(TOKENS, HEADS))

def key_pass(q_heads, k_heads, v_heads, d_heads, deltas, totals, token_ids):
    att_scale = 1.0 / math.sqrt(HEAD)

    def one_block(index):
        start, lower, window = window_bounds(index)
        k_part = lax.dynamic_slice_in_dim(k_heads, start, TOK_DEV, 0)
        v_part = lax.dynamic_slice_in_dim(v_heads, start, TOK_DEV, 0)
        ids_part = lax.dynamic_slice_in_dim(token_ids, start, TOK_DEV, 0)
        q_win = lax.dynamic_slice_in_dim(q_heads, lower, window, 0)
        d_win = lax.dynamic_slice_in_dim(d_heads, lower, window, 0)
        delta_win = lax.dynamic_slice_in_dim(deltas, lower, window, 0)
        total_win = lax.dynamic_slice_in_dim(totals, lower, window, 0)
        ids_win = lax.dynamic_slice_in_dim(token_ids, lower, window, 0)
        linked = ids_win[:, None] == ids_part[None, :]
        scores = jnp.einsum('qhd,khd->hqk', q_win, k_part) * att_scale
        expo = jnp.where(linked[None], jnp.exp(scores), 0.0)
        probs = expo / total_win.T[:, :, None]
        d_prob = jnp.einsum('qhd,khd->hqk', d_win, v_part)
        d_score = round_trip(probs * (d_prob - delta_win.T[:, :, None]))
        probs_bf = round_trip(probs)
        value_sum = jnp.einsum('hqk,qhd->khd', probs_bf, d_win)
        key_sum = att_scale * jnp.einsum('hqk,qhd->khd', d_score, q_win)
        return (key_sum.astype(jnp.bfloat16), value_sum.astype(jnp.bfloat16))
    key_grads, value_grads = lax.map(one_block, jnp.arange(TOKENS // TOK_DEV, dtype=jnp.int32))
    return (key_grads.reshape(TOKENS, FEATS), value_grads.reshape(TOKENS, FEATS))

def reference(queries, keys, values, outputs, out_grad, out_weight, slide_table):
    weight_sum = jnp.zeros((FEATS, D), jnp.float32)
    query_list, key_list, value_list = ([], [], [])
    for replica in range(N_REP):
        attn_grad = jnp.dot(out_grad[replica], out_weight.T, preferred_element_type=jnp.float32).astype(jnp.bfloat16)
        weight_sum = weight_sum + jnp.dot(outputs[replica].T, out_grad[replica], preferred_element_type=jnp.float32)
        d_flat = attn_grad.astype(jnp.float32)
        deltas = lax.optimization_barrier(jnp.sum((d_flat * outputs[replica].astype(jnp.float32)).reshape(TOKENS, HEADS, HEAD), axis=2))
        token_ids = jnp.repeat(slide_table[replica], BLOCK).astype(jnp.int32)
        q_heads = queries[replica].astype(jnp.float32).reshape(TOKENS, HEADS, HEAD)
        k_heads = keys[replica].astype(jnp.float32).reshape(TOKENS, HEADS, HEAD)
        v_heads = values[replica].astype(jnp.float32).reshape(TOKENS, HEADS, HEAD)
        d_heads = d_flat.reshape(TOKENS, HEADS, HEAD)
        query_grad, totals = query_pass(q_heads, k_heads, v_heads, d_heads, deltas, token_ids)
        key_grad, value_grad = key_pass(q_heads, k_heads, v_heads, d_heads, deltas, totals, token_ids)
        query_list.append(query_grad)
        key_list.append(key_grad)
        value_list.append(value_grad)
    weight_grad = weight_sum / math.sqrt(N_REP * TOKENS)
    return (jnp.stack(query_list), jnp.stack(key_list), jnp.stack(value_list), weight_grad)
```

```python
import functools
import math

import jax
import jax.numpy as jnp
from jax import lax
from jax.experimental import pallas as pl
from jax.experimental.pallas import tpu as pltpu
from jax.sharding import PartitionSpec as P

HEAD = 64
UNIT = 128
PAIR = 128
ROWS = 256
FEATS = 384
WIDTH = 768
PAIRS = FEATS // PAIR
HALF = FEATS // 2
TILE = 16
TILES = HALF * WIDTH // (TILE * 128)
GRID = (4, 2, 8, 2, 2)
FAR = -1e30
MESH = pl.DeviceIdType.MESH
F32 = jnp.float32
BF16 = jnp.bfloat16


def nt(a, b):
    return lax.dot_general(a, b, (((1,), (1,)), ((), ())), preferred_element_type=F32)


def nn(a, b):
    return lax.dot_general(a, b, (((1,), (0,)), ((), ())), preferred_element_type=F32)


def roll_half(x):
    return jnp.concatenate([x[:, HEAD:], x[:, :HEAD]], axis=1)


def lanes(shape):
    return lax.broadcasted_iota(jnp.int32, shape, 1)


def below(limit, x, y):
    return jnp.where(lanes(x.shape) < limit, x, y)


def kernel(
    grid, tab, q, k, v, o, dy, w,
    dq, dk, dv, wg,
    d_own, snd_l, snd_r, rcv_l, rcv_r, del_own, del_sl, del_sr, del_rl, del_rr,
    ret_sl, ret_sr, ret_rl, ret_rr, bias, win, p_buf, s_buf, q_turn,
    term, core_in, plane_out, plane_in, line, final,
    halo_send, halo_recv, del_send, del_recv, ret_send, ret_recv,
    core_send, core_recv, plane_send, plane_recv, line_send, line_recv,
    share_send, share_recv, swap_send, swap_recv,
):
    nx, nyl, nz, nyh, ncore = grid
    ny = nyl * nyh
    nplane = nx * ny
    depth = -(-TILES // nplane) * TILE
    nseq = nx * nyl * nz
    seq = lax.axis_index("seq")
    rep = lax.axis_index("rep")
    z = lax.rem(seq, nz)
    yl = lax.rem(seq // nz, nyl)
    x = seq // (nz * nyl)
    core = lax.rem(rep, ncore)
    yh = rep // ncore
    spot = x * ny + yh * nyl + yl
    left = lax.rem(seq + nseq - 1, nseq)
    right = lax.rem(seq + 1, nseq)
    to_left = (left, rep)
    to_right = (right, rep)
    to_core = (seq, yh * ncore + (ncore - 1 - core))

    def plane_peer(offset):
        other = lax.rem(spot + offset, nplane)
        oy = lax.rem(other, ny)
        device = ((other // ny) * nyl + lax.rem(oy, nyl)) * nz + z, (oy // nyl) * ncore + core
        return other, device

    def line_peer(offset):
        return ((seq - z) + lax.rem(z + offset, nz), rep)

    barrier = pltpu.get_barrier_semaphore()
    for peer in (to_left, to_right, to_core):
        pl.semaphore_signal(barrier, inc=1, device_id=peer, device_id_type=MESH)
    for offset in range(1, nplane):
        pl.semaphore_signal(barrier, inc=1, device_id=plane_peer(offset)[1], device_id_type=MESH)
    for offset in range(1, nz):
        pl.semaphore_signal(barrier, inc=1, device_id=line_peer(offset), device_id_type=MESH)

    first = 2 * seq
    last_unit = 2 * nseq - 1

    def unit(step):
        return tab[0, jnp.clip(first + step, 0, last_unit)]

    flag = lambda cond: jnp.where(cond, 1, 0)
    l2, l1, a, b, r1, r2 = (unit(step) for step in (-2, -1, 0, 1, 2, 3))
    ab = flag(a == b)
    l21 = flag(l2 == l1)
    r12 = flag(r1 == r2)
    cross_l = flag(l1 == a) * flag(seq > 0)
    cross_r = flag(b == r1) * flag(seq < nseq - 1)
    split_r = cross_l * ab * l21
    split_l = cross_r * ab * r12
    recv_l = cross_l * ab * (1 - l21)
    sent_l = cross_l * (1 - ab)
    sent_r = cross_r * (1 - ab) * r12
    recv_r = cross_r * (1 - r12)

    low = lambda cond: HEAD * cond
    high = lambda cond: 2 * HEAD - HEAD * cond
    pick = lambda cond, yes, no: jnp.where(cond > 0, yes, no)

    def low_from(cond, x, y):
        return below(low(cond), roll_half(y), x)

    def high_from(cond, x, y):
        return below(high(cond), x, roll_half(y))

    def copy(src, dst, send, recv, peer):
        return pltpu.make_async_remote_copy(
            src_ref=src, dst_ref=dst, send_sem=send, recv_sem=recv,
            device_id=peer, device_id_type=MESH,
        )

    d_own[...] = nt(dy[0], w[...]).astype(BF16)
    prod = d_own[...].astype(F32) * o[0].astype(F32)
    upper = prod.astype(BF16)
    lower = (prod - upper.astype(F32)).astype(BF16)
    chooser = (
        lax.broadcasted_iota(jnp.int32, (8, FEATS), 1) // HEAD
        == lax.broadcasted_iota(jnp.int32, (8, FEATS), 0)
    ).astype(F32).astype(BF16)
    del_own[...] = nt(chooser, upper) + nt(chooser, lower)

    for h in range(2 * PAIRS):
        even = h - h % 2
        da, db = del_own[h:h + 1, :UNIT], del_own[h:h + 1, UNIT:]
        if h % 2:
            db_even = del_own[even:even + 1, UNIT:]
            del_sl[h:h + 1] = below(UNIT * split_r, db_even, da)
            del_sr[h:h + 1] = db
        else:
            da_odd = del_own[h + 1:h + 2, :UNIT]
            del_sl[h:h + 1] = da
            del_sr[h:h + 1] = below(UNIT * split_l, da_odd, db)
    del_sl[6:8] = jnp.zeros((2, UNIT), F32)
    del_sr[6:8] = jnp.zeros((2, UNIT), F32)

    sources = (q, k, v, None)
    for p in range(PAIRS):
        cols = slice(p * PAIR, (p + 1) * PAIR)
        for i, src in enumerate(sources):
            if src is None:
                ua, ub = d_own[:UNIT, cols], d_own[UNIT:, cols]
            else:
                ua, ub = src[0, :UNIT, cols], src[0, UNIT:, cols]
            snd_l[p, i] = high_from(split_r, ua, ub)
            snd_r[p, i] = low_from(split_l, ub, ua)

    for j in range(WIDTH // 128):
        block = lax.dot_general(
            o[0], dy[0, :, j * 128:(j + 1) * 128],
            (((0,), (0,)), ((), ())), preferred_element_type=F32,
        ).astype(BF16)
        for h in range(2):
            term[h, j * HALF:(j + 1) * HALF] = block[h * HALF:(h + 1) * HALF]

    pl.semaphore_wait(barrier, 3 + (nplane - 1) + (nz - 1))

    sends = []

    def go(c):
        c.start()
        sends.append(c)
        return c

    deltas_in = [
        go(copy(del_sl, del_rr, del_send.at[0], del_recv.at[0], to_left)),
        go(copy(del_sr, del_rl, del_send.at[1], del_recv.at[1], to_right)),
    ]
    halo_in = []
    for p in range(PAIRS):
        halo_in.append([
            go(copy(snd_l.at[p], rcv_r.at[p], halo_send.at[0, p], halo_recv.at[0, p], to_left)),
            go(copy(snd_r.at[p], rcv_l.at[p], halo_send.at[1, p], halo_recv.at[1, p], to_right)),
        ])
        if p == 0:
            core_copy = go(copy(term.at[1 - core], core_in, core_send, core_recv, to_core))

    for par in range(2):
        mine_away = split_l if par else split_r
        theirs = split_r if par else split_l
        kinds = (
            pick(recv_l + theirs, a, -3),
            pick(sent_l + mine_away, -1, a),
            pick(sent_r + mine_away, -2, b),
            pick(recv_r + theirs, b, -4),
        )
        for i in range(4):
            for j in range(4):
                level = jnp.where(kinds[i] == kinds[j], F32(-2.0), F32(FAR))
                bias[par, i * UNIT:(i + 1) * UNIT, j * UNIT:(j + 1) * UNIT] = jnp.full(
                    (UNIT, UNIT), level, F32
                )

    core_copy.wait_recv()
    plane_out[...] = (term[core].astype(F32) + core_in[...].astype(F32)).astype(BF16)

    def chunk(index):
        return pl.ds(pl.multiple_of((index * TILES) // nplane * TILE, TILE), depth)

    plane_copies = []
    for offset in range(1, nplane):
        other, peer = plane_peer(offset)
        plane_copies.append(go(copy(
            plane_out.at[chunk(other)], plane_in.at[offset - 1],
            plane_send.at[offset - 1], plane_recv.at[offset - 1], peer,
        )))

    scale = 0.125 * math.log2(math.e)

    def attend(p):
        for c in halo_in[p]:
            c.wait_recv()
        cols = slice(p * PAIR, (p + 1) * PAIR)
        for i, src in enumerate(sources):
            win[i, :UNIT] = low_from(split_l, rcv_l[p, i], rcv_r[p, i])
            win[i, UNIT:3 * UNIT] = d_own[:, cols] if src is None else src[0, :, cols]
            win[i, 3 * UNIT:] = high_from(split_r, rcv_r[p, i], rcv_l[p, i])
        key_turn = win[1].T
        d_keys, d_values = [], []
        for par in range(2):
            h = 2 * p + par
            own = del_own[h:h + 1]
            if par:
                d0 = del_rl[h:h + 1]
                d3 = below(UNIT * split_r, del_rl[h - 1:h], del_rr[h:h + 1])
                zero = jnp.zeros_like(win[1])
                key_one = below(HEAD, zero, win[1])
                value_one = below(HEAD, zero, win[2])
            else:
                d0 = below(UNIT * split_l, del_rr[h + 1:h + 2], del_rl[h:h + 1])
                d3 = del_rr[h:h + 1]
                zero = jnp.zeros_like(win[1])
                key_one = below(HEAD, win[1], zero)
                value_one = below(HEAD, win[2], zero)
            delta_halves = (
                jnp.concatenate([d0, own[:, :UNIT]], axis=1),
                jnp.concatenate([own[:, UNIT:], d3], axis=1),
            )
            for half in range(2):
                part = slice(half * 256, half * 256 + 256)
                scores = nt(key_one, win[0, part])
                expo = jnp.exp2(scores * scale + bias[par, :, part])
                totals = jnp.sum(expo, axis=0, keepdims=True)
                probs = expo * (1.0 / totals)
                d_prob = nt(value_one, win[3, part])
                d_score = (probs * (d_prob - delta_halves[half])).astype(BF16)
                p_buf[:, part] = probs.astype(BF16)
                s_buf[:, part] = d_score
                q_turn[par * HEAD:(par + 1) * HEAD, part] = nn(
                    key_turn[par * HEAD:(par + 1) * HEAD], d_score
                )
            d_values.append(nn(p_buf[...], win[3]))
            d_keys.append(nn(s_buf[...], win[0]))
        grads = (
            (dq, 0.125 * q_turn[...].T),
            (dk, 0.125 * below(HEAD, d_keys[0], d_keys[1])),
            (dv, below(HEAD, d_values[0], d_values[1])),
        )
        for i, (out, grad) in enumerate(grads):
            grad = grad.astype(BF16)
            out[0, :, cols] = grad[UNIT:3 * UNIT]
            before, after = grad[:UNIT], grad[3 * UNIT:]
            ret_sl[p, i] = low_from(split_r, before, after)
            ret_sr[p, i] = high_from(split_l, after, before)
        return [
            go(copy(ret_sl.at[p], ret_rr.at[p], ret_send.at[0, p], ret_recv.at[0, p], to_left)),
            go(copy(ret_sr.at[p], ret_rl.at[p], ret_send.at[1, p], ret_recv.at[1, p], to_right)),
        ]

    for c in deltas_in:
        c.wait_recv()
    returns = [attend(0)]

    for c in plane_copies:
        c.wait_recv()
    total = plane_out[chunk(spot)].astype(F32)
    for offset in range(1, nplane):
        total = total + plane_in[offset - 1].astype(F32)
    line[z] = total.astype(BF16)
    line_copies = []
    for offset in range(1, nz):
        line_copies.append(go(copy(
            line.at[z], line.at[z], line_send.at[offset - 1], line_recv.at[offset - 1],
            line_peer(offset),
        )))

    returns.append(attend(1))

    for c in line_copies:
        c.wait_recv()
    total = line[0].astype(F32)
    for index in range(1, nz):
        total = total + line[index].astype(F32)
    norm = 1.0 / math.sqrt(nseq * ROWS * nyh * ncore)
    final[core, spot] = (total * norm).astype(BF16)
    share_copies = []
    for offset in range(1, nplane):
        _, peer = plane_peer(offset)
        share_copies.append(go(copy(
            final.at[core, spot], final.at[core, spot],
            share_send.at[offset - 1], share_recv.at[offset - 1], peer,
        )))

    returns.append(attend(2))

    for c in share_copies:
        c.wait_recv()
    swap = go(copy(final.at[core], final.at[core], swap_send, swap_recv, to_core))

    for p in range(PAIRS):
        for c in returns[p]:
            c.wait_recv()
        cols = slice(p * PAIR, (p + 1) * PAIR)
        for i, out in enumerate((dq, dk, dv)):
            from_l, from_r = ret_rl[p, i], ret_rr[p, i]
            ua, ub = out[0, :UNIT, cols], out[0, UNIT:, cols]
            ua = high_from(split_l, ua, from_r)
            out[0, :UNIT, cols] = below(HEAD * (2 * sent_l + split_r), from_l, ua)
            ub = low_from(split_r, ub, from_l)
            out[0, UNIT:, cols] = below(
                2 * HEAD - HEAD * (2 * sent_r + split_l), ub, from_r
            )

    swap.wait_recv()
    for h in range(2):
        for index in range(nplane):
            begin = (index * TILES) // nplane
            end = ((index + 1) * TILES) // nplane
            for t in range(begin, end):
                j, row = divmod(t * TILE, HALF)
                wg[h * HALF + row:h * HALF + row + TILE, j * 128:(j + 1) * 128] = final[
                    h, index, (t - begin) * TILE:(t - begin + 1) * TILE
                ].astype(F32)

    for c in sends:
        c.wait_send()


def shards(grid, queries, keys, values, outputs, out_grad, out_weight, slide_table):
    nx, nyl, nz, nyh, ncore = grid
    nplane = nx * nyl * nyh
    depth = -(-TILES // nplane) * TILE
    dma = pltpu.SemaphoreType.DMA
    vmem = pl.BlockSpec(memory_space=pltpu.VMEM)
    part = (1, ROWS, FEATS)
    halo = (PAIRS, 4, UNIT, PAIR)
    back = (PAIRS, 3, UNIT, PAIR)
    return pl.pallas_call(
        functools.partial(kernel, grid),
        out_shape=[jax.ShapeDtypeStruct(part, BF16)] * 3
        + [jax.ShapeDtypeStruct((FEATS, WIDTH), F32)],
        in_specs=[pl.BlockSpec(memory_space=pltpu.SMEM)] + [vmem] * 6,
        out_specs=[vmem] * 4,
        scratch_shapes=[
            pltpu.VMEM((ROWS, FEATS), BF16),
            pltpu.VMEM(halo, BF16),
            pltpu.VMEM(halo, BF16),
            pltpu.VMEM(halo, BF16),
            pltpu.VMEM(halo, BF16),
            pltpu.VMEM((8, ROWS), F32),
            pltpu.VMEM((8, UNIT), F32),
            pltpu.VMEM((8, UNIT), F32),
            pltpu.VMEM((8, UNIT), F32),
            pltpu.VMEM((8, UNIT), F32),
            pltpu.VMEM(back, BF16),
            pltpu.VMEM(back, BF16),
            pltpu.VMEM(back, BF16),
            pltpu.VMEM(back, BF16),
            pltpu.VMEM((2, 4 * UNIT, 4 * UNIT), F32),
            pltpu.VMEM((4, 4 * UNIT, PAIR), BF16),
            pltpu.VMEM((4 * UNIT, 4 * UNIT), BF16),
            pltpu.VMEM((4 * UNIT, 4 * UNIT), BF16),
            pltpu.VMEM((PAIR, 4 * UNIT), F32),
            pltpu.VMEM((2, TILES * TILE, 128), BF16),
            pltpu.VMEM((TILES * TILE, 128), BF16),
            pltpu.VMEM((TILES * TILE, 128), BF16),
            pltpu.VMEM((nplane - 1, depth, 128), BF16),
            pltpu.VMEM((nz, depth, 128), BF16),
            pltpu.VMEM((2, nplane, depth, 128), BF16),
            dma((2, PAIRS)), dma((2, PAIRS)),
            dma((2,)), dma((2,)),
            dma((2, PAIRS)), dma((2, PAIRS)),
            dma, dma,
            dma((nplane - 1,)), dma((nplane - 1,)),
            dma((nz - 1,)), dma((nz - 1,)),
            dma((nplane - 1,)), dma((nplane - 1,)),
            dma, dma,
        ],
        compiler_params=pltpu.CompilerParams(
            collective_id=0, has_side_effects=True, vmem_limit_bytes=48 * 1024 * 1024
        ),
        name="attention_backward",
    )(slide_table, queries, keys, values, outputs, out_grad, out_weight)


def solution(mesh):
    rows = P("rep", "seq", None)
    return jax.shard_map(
        functools.partial(shards, GRID),
        mesh=mesh,
        in_specs=(rows, rows, rows, rows, rows, P(), P("rep", None)),
        out_specs=(rows, rows, rows, P()),
        check_vma=False,
    )
```

```python
import functools
import math

import jax
import jax.numpy as jnp
from jax import lax
from jax.experimental import pallas as pl
from jax.experimental.pallas import tpu as pltpu
from jax.sharding import PartitionSpec as P

HEAD = 64
UNIT = 128
PAIR = 128
ROWS = 256
FEATS = 384
WIDTH = 768
PAIRS = FEATS // PAIR
HALF = FEATS // 2
TILE = 16
TILES = HALF * WIDTH // (TILE * 128)
GRID = (4, 2, 8, 2, 2)
FAR = -1e30
MESH = pl.DeviceIdType.MESH
F32 = jnp.float32
BF16 = jnp.bfloat16


def nt(a, b):
    return lax.dot_general(a, b, (((1,), (1,)), ((), ())), preferred_element_type=F32)


def nn(a, b):
    return lax.dot_general(a, b, (((1,), (0,)), ((), ())), preferred_element_type=F32)


def roll_half(x):
    return jnp.concatenate([x[:, HEAD:], x[:, :HEAD]], axis=1)


def lanes(shape):
    return lax.broadcasted_iota(jnp.int32, shape, 1)


def below(limit, x, y):
    return jnp.where(lanes(x.shape) < limit, x, y)


def kernel(
    grid, tab, q_in, k_in, v_in, o_in, dy_in, w_in,
    dq_out, dk_out, dv_out, final_out,
    q, k, v, o, dy, w, load_sem, dq, dk, dv, final, out_sem,
    d_own, snd_l, snd_r, rcv_l, rcv_r, del_own, del_sl, del_sr, del_rl, del_rr,
    ret_sl, ret_sr, ret_rl, ret_rr, bias, win, p_buf, s_buf, q_turn,
    term, core_in, plane_out, plane_in, line,
    halo_send, halo_recv, del_send, del_recv, ret_send, ret_recv,
    core_send, core_recv, plane_send, plane_recv, line_send, line_recv,
    share_send, share_recv, swap_send, swap_recv,
):
    nx, nyl, nz, nyh, ncore = grid
    ny = nyl * nyh
    nplane = nx * ny
    depth = -(-TILES // nplane) * TILE
    nseq = nx * nyl * nz
    seq = lax.axis_index("seq")
    rep = lax.axis_index("rep")
    z = lax.rem(seq, nz)
    yl = lax.rem(seq // nz, nyl)
    x = seq // (nz * nyl)
    core = lax.rem(rep, ncore)
    yh = rep // ncore
    spot = x * ny + yh * nyl + yl
    left = lax.rem(seq + nseq - 1, nseq)
    right = lax.rem(seq + 1, nseq)
    to_left = (left, rep)
    to_right = (right, rep)
    to_core = (seq, yh * ncore + (ncore - 1 - core))

    def plane_peer(offset):
        other = lax.rem(spot + offset, nplane)
        oy = lax.rem(other, ny)
        device = ((other // ny) * nyl + lax.rem(oy, nyl)) * nz + z, (oy // nyl) * ncore + core
        return other, device

    def line_peer(offset):
        return ((seq - z) + lax.rem(z + offset, nz), rep)

    barrier = pltpu.get_barrier_semaphore()
    for peer in (to_left, to_right, to_core):
        pl.semaphore_signal(barrier, inc=1, device_id=peer, device_id_type=MESH)
    for offset in range(1, nplane):
        pl.semaphore_signal(barrier, inc=1, device_id=plane_peer(offset)[1], device_id_type=MESH)
    for offset in range(1, nz):
        pl.semaphore_signal(barrier, inc=1, device_id=line_peer(offset), device_id_type=MESH)

    loads = [
        pltpu.make_async_copy(src, dst, load_sem.at[i])
        for i, (src, dst) in enumerate(
            ((dy_in, dy), (w_in, w), (o_in, o), (q_in, q), (k_in, k), (v_in, v))
        )
    ]
    for c in loads:
        c.start()

    first = 2 * seq
    last_unit = 2 * nseq - 1

    def unit(step):
        return tab[0, jnp.clip(first + step, 0, last_unit)]

    flag = lambda cond: jnp.where(cond, 1, 0)
    l2, l1, a, b, r1, r2 = (unit(step) for step in (-2, -1, 0, 1, 2, 3))
    ab = flag(a == b)
    l21 = flag(l2 == l1)
    r12 = flag(r1 == r2)
    cross_l = flag(l1 == a) * flag(seq > 0)
    cross_r = flag(b == r1) * flag(seq < nseq - 1)
    split_r = cross_l * ab * l21
    split_l = cross_r * ab * r12
    recv_l = cross_l * ab * (1 - l21)
    sent_l = cross_l * (1 - ab)
    sent_r = cross_r * (1 - ab) * r12
    recv_r = cross_r * (1 - r12)

    low = lambda cond: HEAD * cond
    high = lambda cond: 2 * HEAD - HEAD * cond
    pick = lambda cond, yes, no: jnp.where(cond > 0, yes, no)

    def low_from(cond, x, y):
        return below(low(cond), roll_half(y), x)

    def high_from(cond, x, y):
        return below(high(cond), x, roll_half(y))

    def copy(src, dst, send, recv, peer):
        return pltpu.make_async_remote_copy(
            src_ref=src, dst_ref=dst, send_sem=send, recv_sem=recv,
            device_id=peer, device_id_type=MESH,
        )

    for c in loads[:3]:
        c.wait()
    d_own[...] = nt(dy[0], w[...]).astype(BF16)
    prod = d_own[...].astype(F32) * o[0].astype(F32)
    upper = prod.astype(BF16)
    lower = (prod - upper.astype(F32)).astype(BF16)
    chooser = (
        lax.broadcasted_iota(jnp.int32, (8, FEATS), 1) // HEAD
        == lax.broadcasted_iota(jnp.int32, (8, FEATS), 0)
    ).astype(F32).astype(BF16)
    del_own[...] = nt(chooser, upper) + nt(chooser, lower)

    for h in range(2 * PAIRS):
        even = h - h % 2
        da, db = del_own[h:h + 1, :UNIT], del_own[h:h + 1, UNIT:]
        if h % 2:
            db_even = del_own[even:even + 1, UNIT:]
            del_sl[h:h + 1] = below(UNIT * split_r, db_even, da)
            del_sr[h:h + 1] = db
        else:
            da_odd = del_own[h + 1:h + 2, :UNIT]
            del_sl[h:h + 1] = da
            del_sr[h:h + 1] = below(UNIT * split_l, da_odd, db)
    del_sl[6:8] = jnp.zeros((2, UNIT), F32)
    del_sr[6:8] = jnp.zeros((2, UNIT), F32)

    for c in loads[3:]:
        c.wait()
    sources = (q, k, v, None)
    for p in range(PAIRS):
        cols = slice(p * PAIR, (p + 1) * PAIR)
        for i, src in enumerate(sources):
            if src is None:
                ua, ub = d_own[:UNIT, cols], d_own[UNIT:, cols]
            else:
                ua, ub = src[0, :UNIT, cols], src[0, UNIT:, cols]
            snd_l[p, i] = high_from(split_r, ua, ub)
            snd_r[p, i] = low_from(split_l, ub, ua)

    for j in range(WIDTH // 128):
        block = lax.dot_general(
            o[0], dy[0, :, j * 128:(j + 1) * 128],
            (((0,), (0,)), ((), ())), preferred_element_type=F32,
        ).astype(BF16)
        for h in range(2):
            term[h, j * HALF:(j + 1) * HALF] = block[h * HALF:(h + 1) * HALF]

    pl.semaphore_wait(barrier, 3 + (nplane - 1) + (nz - 1))

    sends = []

    def go(c):
        c.start()
        sends.append(c)
        return c

    deltas_in = [
        go(copy(del_sl, del_rr, del_send.at[0], del_recv.at[0], to_left)),
        go(copy(del_sr, del_rl, del_send.at[1], del_recv.at[1], to_right)),
    ]
    halo_l = [
        copy(snd_l.at[p], rcv_r.at[p], halo_send.at[0, p], halo_recv.at[0, p], to_left)
        for p in range(PAIRS)
    ]
    halo_r = [
        copy(snd_r.at[p], rcv_l.at[p], halo_send.at[1, p], halo_recv.at[1, p], to_right)
        for p in range(PAIRS)
    ]
    edge_l, edge_r = z == 0, z == nz - 1

    def forward(p, edges):
        for c, edge in ((halo_l[p], edge_l), (halo_r[p], edge_r)):
            if edges is None:
                c.start()
            else:
                pl.when(edge if edges else jnp.logical_not(edge))(c.start)

    core_copy = go(copy(term.at[1 - core], core_in, core_send, core_recv, to_core))
    forward(0, None)

    for par in range(2):
        mine_away = split_l if par else split_r
        theirs = split_r if par else split_l
        kinds = (
            pick(recv_l + theirs, a, -3),
            pick(sent_l + mine_away, -1, a),
            pick(sent_r + mine_away, -2, b),
            pick(recv_r + theirs, b, -4),
        )
        for i in range(4):
            for j in range(4):
                level = jnp.where(kinds[i] == kinds[j], F32(-2.0), F32(FAR))
                bias[par, i * UNIT:(i + 1) * UNIT, j * UNIT:(j + 1) * UNIT] = jnp.full(
                    (UNIT, UNIT), level, F32
                )

    core_copy.wait_recv()
    plane_out[...] = (term[core].astype(F32) + core_in[...].astype(F32)).astype(BF16)

    def chunk(index):
        return pl.ds(pl.multiple_of((index * TILES) // nplane * TILE, TILE), depth)

    plane_copies = []
    for offset in range(1, nplane):
        other, peer = plane_peer(offset)
        plane_copies.append(go(copy(
            plane_out.at[chunk(other)], plane_in.at[offset - 1],
            plane_send.at[offset - 1], plane_recv.at[offset - 1], peer,
        )))

    forward(1, False)

    scale = 0.125 * math.log2(math.e)

    def arrive(p):
        halo_l[p].wait_recv()
        halo_r[p].wait_recv()

    def attend(p):
        cols = slice(p * PAIR, (p + 1) * PAIR)
        for i, src in enumerate(sources):
            win[i, :UNIT] = low_from(split_l, rcv_l[p, i], rcv_r[p, i])
            win[i, UNIT:3 * UNIT] = d_own[:, cols] if src is None else src[0, :, cols]
            win[i, 3 * UNIT:] = high_from(split_r, rcv_r[p, i], rcv_l[p, i])
        key_turn = win[1].T
        d_keys, d_values = [], []
        for par in range(2):
            h = 2 * p + par
            own = del_own[h:h + 1]
            if par:
                d0 = del_rl[h:h + 1]
                d3 = below(UNIT * split_r, del_rl[h - 1:h], del_rr[h:h + 1])
                zero = jnp.zeros_like(win[1])
                key_one = below(HEAD, zero, win[1])
                value_one = below(HEAD, zero, win[2])
            else:
                d0 = below(UNIT * split_l, del_rr[h + 1:h + 2], del_rl[h:h + 1])
                d3 = del_rr[h:h + 1]
                zero = jnp.zeros_like(win[1])
                key_one = below(HEAD, win[1], zero)
                value_one = below(HEAD, win[2], zero)
            delta_halves = (
                jnp.concatenate([d0, own[:, :UNIT]], axis=1),
                jnp.concatenate([own[:, UNIT:], d3], axis=1),
            )
            for half in range(2):
                part = slice(half * 256, half * 256 + 256)
                scores = nt(key_one, win[0, part])
                expo = jnp.exp2(scores * scale + bias[par, :, part])
                totals = jnp.sum(expo, axis=0, keepdims=True)
                probs = expo * (1.0 / totals)
                d_prob = nt(value_one, win[3, part])
                d_score = (probs * (d_prob - delta_halves[half])).astype(BF16)
                p_buf[:, part] = probs.astype(BF16)
                s_buf[:, part] = d_score
                q_turn[par * HEAD:(par + 1) * HEAD, part] = nn(
                    key_turn[par * HEAD:(par + 1) * HEAD], d_score
                )
            d_values.append(nn(p_buf[...], win[3]))
            d_keys.append(nn(s_buf[...], win[0]))
        grads = (
            (dq, 0.125 * q_turn[...].T),
            (dk, 0.125 * below(HEAD, d_keys[0], d_keys[1])),
            (dv, below(HEAD, d_values[0], d_values[1])),
        )
        for i, (out, grad) in enumerate(grads):
            grad = grad.astype(BF16)
            out[0, :, cols] = grad[UNIT:3 * UNIT]
            before, after = grad[:UNIT], grad[3 * UNIT:]
            ret_sl[p, i] = low_from(split_r, before, after)
            ret_sr[p, i] = high_from(split_l, after, before)

    returns = []

    def give_back(p):
        returns.append([
            go(copy(ret_sl.at[p], ret_rr.at[p], ret_send.at[0, p], ret_recv.at[0, p], to_left)),
            go(copy(ret_sr.at[p], ret_rl.at[p], ret_send.at[1, p], ret_recv.at[1, p], to_right)),
        ])

    for c in deltas_in:
        c.wait_recv()
    arrive(0)
    forward(2, False)
    forward(1, True)
    attend(0)
    forward(2, True)

    for c in plane_copies:
        c.wait_recv()
    total = plane_out[chunk(spot)].astype(F32)
    for offset in range(1, nplane):
        total = total + plane_in[offset - 1].astype(F32)
    line[z] = total.astype(BF16)
    line_copies = []
    for offset in range(1, nz):
        line_copies.append(go(copy(
            line.at[z], line.at[z], line_send.at[offset - 1], line_recv.at[offset - 1],
            line_peer(offset),
        )))

    give_back(0)
    arrive(1)
    attend(1)
    give_back(1)

    for c in line_copies:
        c.wait_recv()
    total = line[0].astype(F32)
    for index in range(1, nz):
        total = total + line[index].astype(F32)
    norm = 1.0 / math.sqrt(nseq * ROWS * nyh * ncore)
    final[core, spot] = (total * norm).astype(BF16)
    share_copies = []
    for offset in range(1, nplane):
        _, peer = plane_peer(offset)
        share_copies.append(go(copy(
            final.at[core, spot], final.at[core, spot],
            share_send.at[offset - 1], share_recv.at[offset - 1], peer,
        )))

    arrive(2)
    attend(2)
    give_back(2)

    for p in range(PAIRS):
        for c in returns[p]:
            c.wait_recv()
        cols = slice(p * PAIR, (p + 1) * PAIR)
        for i, out in enumerate((dq, dk, dv)):
            from_l, from_r = ret_rl[p, i], ret_rr[p, i]
            ua, ub = out[0, :UNIT, cols], out[0, UNIT:, cols]
            ua = high_from(split_l, ua, from_r)
            out[0, :UNIT, cols] = below(HEAD * (2 * sent_l + split_r), from_l, ua)
            ub = low_from(split_r, ub, from_l)
            out[0, UNIT:, cols] = below(
                2 * HEAD - HEAD * (2 * sent_r + split_l), ub, from_r
            )

    writes = [
        pltpu.make_async_copy(src, dst, out_sem.at[i])
        for i, (src, dst) in enumerate(((dq, dq_out), (dk, dk_out), (dv, dv_out)))
    ]
    for c in writes:
        c.start()

    for c in share_copies:
        c.wait_recv()
    swap = go(copy(final.at[core], final.at[core], swap_send, swap_recv, to_core))

    writes.append(pltpu.make_async_copy(final.at[core], final_out.at[core], out_sem.at[3]))
    writes[-1].start()
    swap.wait_recv()
    writes.append(
        pltpu.make_async_copy(final.at[1 - core], final_out.at[1 - core], out_sem.at[4])
    )
    writes[-1].start()
    for c in sends + halo_l + halo_r:
        c.wait_send()
    for c in writes:
        c.wait()


def finish(nplane, dq, dk, dv, total, dq_out, dk_out, dv_out, wg_out, parts, final, wg, sem):
    flows = ((dq, dq_out), (dk, dk_out), (dv, dv_out))
    loads = [
        pltpu.make_async_copy(total.at[h], final.at[h], sem.at[h]) for h in range(2)
    ] + [
        pltpu.make_async_copy(src, parts.at[i], sem.at[2 + i]) for i, (src, _) in enumerate(flows)
    ]
    for c in loads:
        c.start()
    copies = []
    for h in range(2):
        loads[h].wait()
        for index in range(nplane):
            begin = (index * TILES) // nplane
            end = ((index + 1) * TILES) // nplane
            for t in range(begin, end):
                j, row = divmod(t * TILE, HALF)
                wg[h * HALF + row:h * HALF + row + TILE, j * 128:(j + 1) * 128] = final[
                    h, index, (t - begin) * TILE:(t - begin + 1) * TILE
                ].astype(F32)
        rows = pl.ds(h * HALF, HALF)
        copies.append(pltpu.make_async_copy(wg.at[rows], wg_out.at[rows], sem.at[5 + h]))
        copies[-1].start()
    for i, (_, dst) in enumerate(flows):
        loads[2 + i].wait()
        copies.append(pltpu.make_async_copy(parts.at[i], dst, sem.at[7 + i]))
        copies[-1].start()
    for c in copies:
        c.wait()


def shards(grid, queries, keys, values, outputs, out_grad, out_weight, slide_table):
    nx, nyl, nz, nyh, ncore = grid
    nplane = nx * nyl * nyh
    depth = -(-TILES // nplane) * TILE
    dma = pltpu.SemaphoreType.DMA
    part = (1, ROWS, FEATS)
    halo = (PAIRS, 4, UNIT, PAIR)
    back = (PAIRS, 3, UNIT, PAIR)
    parts = pl.pallas_call(
        functools.partial(kernel, grid),
        out_shape=[jax.ShapeDtypeStruct(part, BF16)] * 3
        + [jax.ShapeDtypeStruct((2, nplane, depth, 128), BF16)],
        in_specs=[pl.BlockSpec(memory_space=pltpu.SMEM)] + [pl.BlockSpec(memory_space=pl.ANY)] * 6,
        out_specs=[pl.BlockSpec(memory_space=pl.ANY)] * 4,
        scratch_shapes=[
            *[pltpu.VMEM(part, BF16)] * 4,
            pltpu.VMEM((1, ROWS, WIDTH), BF16),
            pltpu.VMEM((FEATS, WIDTH), BF16),
            dma((6,)),
            *[pltpu.VMEM(part, BF16)] * 3,
            pltpu.VMEM((2, nplane, depth, 128), BF16),
            dma((5,)),
            pltpu.VMEM((ROWS, FEATS), BF16),
            pltpu.VMEM(halo, BF16),
            pltpu.VMEM(halo, BF16),
            pltpu.VMEM(halo, BF16),
            pltpu.VMEM(halo, BF16),
            pltpu.VMEM((8, ROWS), F32),
            pltpu.VMEM((8, UNIT), F32),
            pltpu.VMEM((8, UNIT), F32),
            pltpu.VMEM((8, UNIT), F32),
            pltpu.VMEM((8, UNIT), F32),
            pltpu.VMEM(back, BF16),
            pltpu.VMEM(back, BF16),
            pltpu.VMEM(back, BF16),
            pltpu.VMEM(back, BF16),
            pltpu.VMEM((2, 4 * UNIT, 4 * UNIT), F32),
            pltpu.VMEM((4, 4 * UNIT, PAIR), BF16),
            pltpu.VMEM((4 * UNIT, 4 * UNIT), BF16),
            pltpu.VMEM((4 * UNIT, 4 * UNIT), BF16),
            pltpu.VMEM((PAIR, 4 * UNIT), F32),
            pltpu.VMEM((2, TILES * TILE, 128), BF16),
            pltpu.VMEM((TILES * TILE, 128), BF16),
            pltpu.VMEM((TILES * TILE, 128), BF16),
            pltpu.VMEM((nplane - 1, depth, 128), BF16),
            pltpu.VMEM((nz, depth, 128), BF16),
            dma((2, PAIRS)), dma((2, PAIRS)),
            dma((2,)), dma((2,)),
            dma((2, PAIRS)), dma((2, PAIRS)),
            dma, dma,
            dma((nplane - 1,)), dma((nplane - 1,)),
            dma((nz - 1,)), dma((nz - 1,)),
            dma((nplane - 1,)), dma((nplane - 1,)),
            dma, dma,
        ],
        compiler_params=pltpu.CompilerParams(
            collective_id=0, has_side_effects=True, vmem_limit_bytes=56 * 1024 * 1024
        ),
        name="attention_backward",
    )(slide_table, queries, keys, values, outputs, out_grad, out_weight)
    return pl.pallas_call(
        functools.partial(finish, nplane),
        out_shape=[jax.ShapeDtypeStruct(part, BF16)] * 3
        + [jax.ShapeDtypeStruct((FEATS, WIDTH), F32)],
        in_specs=[pl.BlockSpec(memory_space=pl.ANY)] * 4,
        out_specs=[pl.BlockSpec(memory_space=pl.ANY)] * 4,
        scratch_shapes=[
            pltpu.VMEM((3, *part), BF16),
            pltpu.VMEM((2, nplane, depth, 128), BF16),
            pltpu.VMEM((FEATS, WIDTH), F32),
            dma((10,)),
        ],
        compiler_params=pltpu.CompilerParams(vmem_limit_bytes=56 * 1024 * 1024),
        name="results",
    )(*parts)


def solution(mesh):
    rows = P("rep", "seq", None)
    return jax.shard_map(
        functools.partial(shards, GRID),
        mesh=mesh,
        in_specs=(rows, rows, rows, rows, rows, P(), P("rep", None)),
        out_specs=(rows, rows, rows, P()),
        check_vma=False,
    )
```

```python
import functools
import math

import jax
import jax.numpy as jnp
from jax import lax
from jax.experimental import pallas as pl
from jax.experimental.pallas import tpu as pltpu
from jax.sharding import PartitionSpec as P

HEAD = 64
UNIT = 128
PAIR = 128
ROWS = 256
FEATS = 384
WIDTH = 768
PAIRS = FEATS // PAIR
HALF = FEATS // 2
TILE = 16
TILES = HALF * WIDTH // (TILE * 128)
GRID = (4, 2, 8, 2, 2)
FAR = -1e30
MESH = pl.DeviceIdType.MESH
F32 = jnp.float32
BF16 = jnp.bfloat16


def nt(a, b):
    return lax.dot_general(a, b, (((1,), (1,)), ((), ())), preferred_element_type=F32)


def nn(a, b):
    return lax.dot_general(a, b, (((1,), (0,)), ((), ())), preferred_element_type=F32)


def roll_half(x):
    return jnp.concatenate([x[:, HEAD:], x[:, :HEAD]], axis=1)


def lanes(shape):
    return lax.broadcasted_iota(jnp.int32, shape, 1)


def below(limit, x, y):
    return jnp.where(lanes(x.shape) < limit, x, y)


def kernel(
    grid, tab, q_in, k_in, v_in, o_in, dy_in, w_in,
    dq_out, dk_out, dv_out, final_out,
    q, k, v, o, dy, w, load_sem, dq, dk, dv, final, out_sem,
    d_own, snd_l, snd_r, rcv_l, rcv_r, del_own, del_sl, del_sr, del_rl, del_rr,
    ret_sl, ret_sr, ret_rl, ret_rr, bias, win, p_buf, s_buf, q_turn,
    term, core_in, plane_out, plane_in, line,
    halo_send, halo_recv, del_send, del_recv, ret_send, ret_recv,
    core_send, core_recv, plane_send, plane_recv, line_send, line_recv,
    share_send, share_recv, swap_send, swap_recv,
):
    nx, nyl, nz, nyh, ncore = grid
    ny = nyl * nyh
    nplane = nx * ny
    depth = -(-TILES // nplane) * TILE
    nseq = nx * nyl * nz
    seq = lax.axis_index("seq")
    rep = lax.axis_index("rep")
    z = lax.rem(seq, nz)
    yl = lax.rem(seq // nz, nyl)
    x = seq // (nz * nyl)
    core = lax.rem(rep, ncore)
    yh = rep // ncore
    spot = x * ny + yh * nyl + yl
    left = lax.rem(seq + nseq - 1, nseq)
    right = lax.rem(seq + 1, nseq)
    to_left = (left, rep)
    to_right = (right, rep)
    to_core = (seq, yh * ncore + (ncore - 1 - core))

    def plane_peer(offset):
        other = lax.rem(spot + offset, nplane)
        oy = lax.rem(other, ny)
        device = ((other // ny) * nyl + lax.rem(oy, nyl)) * nz + z, (oy // nyl) * ncore + core
        return other, device

    def line_peer(offset):
        return ((seq - z) + lax.rem(z + offset, nz), rep)

    barrier = pltpu.get_barrier_semaphore()
    for peer in (to_left, to_right, to_core):
        pl.semaphore_signal(barrier, inc=1, device_id=peer, device_id_type=MESH)
    for offset in range(1, nplane):
        pl.semaphore_signal(barrier, inc=1, device_id=plane_peer(offset)[1], device_id_type=MESH)
    for offset in range(1, nz):
        pl.semaphore_signal(barrier, inc=1, device_id=line_peer(offset), device_id_type=MESH)

    loads = [
        pltpu.make_async_copy(src, dst, load_sem.at[i])
        for i, (src, dst) in enumerate(
            ((dy_in, dy), (w_in, w), (o_in, o), (q_in, q), (k_in, k), (v_in, v))
        )
    ]
    for c in loads:
        c.start()

    first = 2 * seq
    last_unit = 2 * nseq - 1

    def unit(step):
        return tab[0, jnp.clip(first + step, 0, last_unit)]

    flag = lambda cond: jnp.where(cond, 1, 0)
    l2, l1, a, b, r1, r2 = (unit(step) for step in (-2, -1, 0, 1, 2, 3))
    ab = flag(a == b)
    l21 = flag(l2 == l1)
    r12 = flag(r1 == r2)
    cross_l = flag(l1 == a) * flag(seq > 0)
    cross_r = flag(b == r1) * flag(seq < nseq - 1)
    split_r = cross_l * ab * l21
    split_l = cross_r * ab * r12
    recv_l = cross_l * ab * (1 - l21)
    sent_l = cross_l * (1 - ab)
    sent_r = cross_r * (1 - ab) * r12
    recv_r = cross_r * (1 - r12)

    low = lambda cond: HEAD * cond
    high = lambda cond: 2 * HEAD - HEAD * cond
    pick = lambda cond, yes, no: jnp.where(cond > 0, yes, no)

    def low_from(cond, x, y):
        return below(low(cond), roll_half(y), x)

    def high_from(cond, x, y):
        return below(high(cond), x, roll_half(y))

    def copy(src, dst, send, recv, peer):
        return pltpu.make_async_remote_copy(
            src_ref=src, dst_ref=dst, send_sem=send, recv_sem=recv,
            device_id=peer, device_id_type=MESH,
        )

    for c in loads[:3]:
        c.wait()
    d_own[...] = nt(dy[0], w[...]).astype(BF16)
    prod = d_own[...].astype(F32) * o[0].astype(F32)
    upper = prod.astype(BF16)
    lower = (prod - upper.astype(F32)).astype(BF16)
    chooser = (
        lax.broadcasted_iota(jnp.int32, (8, FEATS), 1) // HEAD
        == lax.broadcasted_iota(jnp.int32, (8, FEATS), 0)
    ).astype(F32).astype(BF16)
    del_own[...] = nt(chooser, upper) + nt(chooser, lower)

    for h in range(2 * PAIRS):
        even = h - h % 2
        da, db = del_own[h:h + 1, :UNIT], del_own[h:h + 1, UNIT:]
        if h % 2:
            db_even = del_own[even:even + 1, UNIT:]
            del_sl[h:h + 1] = below(UNIT * split_r, db_even, da)
            del_sr[h:h + 1] = db
        else:
            da_odd = del_own[h + 1:h + 2, :UNIT]
            del_sl[h:h + 1] = da
            del_sr[h:h + 1] = below(UNIT * split_l, da_odd, db)
    del_sl[6:8] = jnp.zeros((2, UNIT), F32)
    del_sr[6:8] = jnp.zeros((2, UNIT), F32)

    for c in loads[3:]:
        c.wait()
    sources = (q, k, v, None)
    for p in range(PAIRS):
        cols = slice(p * PAIR, (p + 1) * PAIR)
        for i, src in enumerate(sources):
            if src is None:
                ua, ub = d_own[:UNIT, cols], d_own[UNIT:, cols]
            else:
                ua, ub = src[0, :UNIT, cols], src[0, UNIT:, cols]
            snd_l[p, i] = high_from(split_r, ua, ub)
            snd_r[p, i] = low_from(split_l, ub, ua)

    for j in range(WIDTH // 128):
        block = lax.dot_general(
            o[0], dy[0, :, j * 128:(j + 1) * 128],
            (((0,), (0,)), ((), ())), preferred_element_type=F32,
        ).astype(BF16)
        for h in range(2):
            term[h, j * HALF:(j + 1) * HALF] = block[h * HALF:(h + 1) * HALF]

    pl.semaphore_wait(barrier, 3 + (nplane - 1) + (nz - 1))

    short = TILES // nplane * TILE

    def has_tail(index):
        return ((index + 1) * TILES) // nplane - (index * TILES) // nplane > TILES // nplane

    class Chunk:
        def __init__(self, index, make):
            self.either = ((make(short), jnp.logical_not(has_tail(index))),
                           (make(depth), has_tail(index)))
            if short == depth:
                self.either = ((make(depth), None),)

        def each(self, name):
            for c, cond in self.either:
                if cond is None:
                    getattr(c, name)()
                else:
                    pl.when(cond)(getattr(c, name))

        def start(self):
            self.each("start")

        def wait_recv(self):
            self.each("wait_recv")

        def wait_send(self):
            self.each("wait_send")

    sends = []

    def go(c):
        c.start()
        sends.append(c)
        return c

    deltas_in = [
        go(copy(del_sl, del_rr, del_send.at[0], del_recv.at[0], to_left)),
        go(copy(del_sr, del_rl, del_send.at[1], del_recv.at[1], to_right)),
    ]
    halo_l = [
        copy(snd_l.at[p], rcv_r.at[p], halo_send.at[0, p], halo_recv.at[0, p], to_left)
        for p in range(PAIRS)
    ]
    halo_r = [
        copy(snd_r.at[p], rcv_l.at[p], halo_send.at[1, p], halo_recv.at[1, p], to_right)
        for p in range(PAIRS)
    ]
    edge_l, edge_r = z == 0, z == nz - 1

    def forward(p, edges):
        for c, edge in ((halo_l[p], edge_l), (halo_r[p], edge_r)):
            if edges is None:
                c.start()
            else:
                pl.when(edge if edges else jnp.logical_not(edge))(c.start)

    core_copy = go(copy(term.at[1 - core], core_in, core_send, core_recv, to_core))
    forward(0, None)

    for par in range(2):
        mine_away = split_l if par else split_r
        theirs = split_r if par else split_l
        kinds = (
            pick(recv_l + theirs, a, -3),
            pick(sent_l + mine_away, -1, a),
            pick(sent_r + mine_away, -2, b),
            pick(recv_r + theirs, b, -4),
        )
        for i in range(4):
            for j in range(4):
                level = jnp.where(kinds[i] == kinds[j], F32(-2.0), F32(FAR))
                bias[par, i * UNIT:(i + 1) * UNIT, j * UNIT:(j + 1) * UNIT] = jnp.full(
                    (UNIT, UNIT), level, F32
                )

    core_copy.wait_recv()
    plane_out[...] = (term[core].astype(F32) + core_in[...].astype(F32)).astype(BF16)

    def chunk(index, rows):
        return pl.ds(pl.multiple_of((index * TILES) // nplane * TILE, TILE), rows)

    plane_in_copies = []
    for offset in range(1, nplane):
        other, peer = plane_peer(offset)

        def make(rows, other=other, peer=peer, i=offset - 1):
            return copy(
                plane_out.at[chunk(other, rows)], plane_in.at[i, pl.ds(0, rows)],
                plane_send.at[i], plane_recv.at[i], peer,
            )

        go(Chunk(other, make))
        plane_in_copies.append(Chunk(spot, make))

    forward(1, False)

    scale = 0.125 * math.log2(math.e)

    def arrive(p):
        halo_l[p].wait_recv()
        halo_r[p].wait_recv()

    def attend(p):
        cols = slice(p * PAIR, (p + 1) * PAIR)
        for i, src in enumerate(sources):
            win[i, :UNIT] = low_from(split_l, rcv_l[p, i], rcv_r[p, i])
            win[i, UNIT:3 * UNIT] = d_own[:, cols] if src is None else src[0, :, cols]
            win[i, 3 * UNIT:] = high_from(split_r, rcv_r[p, i], rcv_l[p, i])
        key_turn = win[1].T
        d_keys, d_values = [], []
        for par in range(2):
            h = 2 * p + par
            own = del_own[h:h + 1]
            if par:
                d0 = del_rl[h:h + 1]
                d3 = below(UNIT * split_r, del_rl[h - 1:h], del_rr[h:h + 1])
                zero = jnp.zeros_like(win[1])
                key_one = below(HEAD, zero, win[1])
                value_one = below(HEAD, zero, win[2])
            else:
                d0 = below(UNIT * split_l, del_rr[h + 1:h + 2], del_rl[h:h + 1])
                d3 = del_rr[h:h + 1]
                zero = jnp.zeros_like(win[1])
                key_one = below(HEAD, win[1], zero)
                value_one = below(HEAD, win[2], zero)
            delta_halves = (
                jnp.concatenate([d0, own[:, :UNIT]], axis=1),
                jnp.concatenate([own[:, UNIT:], d3], axis=1),
            )
            for half in range(2):
                part = slice(half * 256, half * 256 + 256)
                scores = nt(key_one, win[0, part])
                expo = jnp.exp2(scores * scale + bias[par, :, part])
                totals = jnp.sum(expo, axis=0, keepdims=True)
                probs = expo * (1.0 / totals)
                d_prob = nt(value_one, win[3, part])
                d_score = (probs * (d_prob - delta_halves[half])).astype(BF16)
                p_buf[:, part] = probs.astype(BF16)
                s_buf[:, part] = d_score
                q_turn[par * HEAD:(par + 1) * HEAD, part] = nn(
                    key_turn[par * HEAD:(par + 1) * HEAD], d_score
                )
            d_values.append(nn(p_buf[...], win[3]))
            d_keys.append(nn(s_buf[...], win[0]))
        grads = (
            (dq, 0.125 * q_turn[...].T),
            (dk, 0.125 * below(HEAD, d_keys[0], d_keys[1])),
            (dv, below(HEAD, d_values[0], d_values[1])),
        )
        for i, (out, grad) in enumerate(grads):
            grad = grad.astype(BF16)
            out[0, :, cols] = grad[UNIT:3 * UNIT]
            before, after = grad[:UNIT], grad[3 * UNIT:]
            ret_sl[p, i] = low_from(split_r, before, after)
            ret_sr[p, i] = high_from(split_l, after, before)

    returns = []

    def give_back(p):
        returns.append([
            go(copy(ret_sl.at[p], ret_rr.at[p], ret_send.at[0, p], ret_recv.at[0, p], to_left)),
            go(copy(ret_sr.at[p], ret_rl.at[p], ret_send.at[1, p], ret_recv.at[1, p], to_right)),
        ])

    for c in deltas_in:
        c.wait_recv()
    arrive(0)
    forward(2, False)
    forward(1, True)
    forward(2, True)
    attend(0)

    for c in plane_in_copies:
        c.wait_recv()
    total = plane_out[chunk(spot, depth)].astype(F32)
    for offset in range(1, nplane):
        total = total + plane_in[offset - 1].astype(F32)
    line[z] = total.astype(BF16)
    line_copies = []
    for offset in range(1, nz):
        line_copies.append(go(Chunk(spot, lambda rows, offset=offset: copy(
            line.at[z, pl.ds(0, rows)], line.at[z, pl.ds(0, rows)],
            line_send.at[offset - 1], line_recv.at[offset - 1], line_peer(offset),
        ))))

    give_back(0)
    arrive(1)
    attend(1)
    give_back(1)

    for c in line_copies:
        c.wait_recv()
    total = line[0].astype(F32)
    for index in range(1, nz):
        total = total + line[index].astype(F32)
    norm = 1.0 / math.sqrt(nseq * ROWS * nyh * ncore)
    final[core, spot] = (total * norm).astype(BF16)

    def passed(index, i):
        def make(rows):
            part = final.at[core, index, pl.ds(0, rows)]
            return copy(part, part, swap_send.at[i], swap_recv.at[i], to_core)
        return Chunk(index, make)

    def shared(index, i, peer):
        def make(rows):
            part = final.at[core, index, pl.ds(0, rows)]
            return copy(part, part, share_send.at[i], share_recv.at[i], peer)
        return Chunk(index, make)

    for offset in range(1, nplane):
        go(shared(spot, offset - 1, plane_peer(offset)[1]))
    go(passed(spot, 0))

    arrive(2)
    attend(2)
    give_back(2)

    for p in range(PAIRS):
        for c in returns[p]:
            c.wait_recv()
        cols = slice(p * PAIR, (p + 1) * PAIR)
        for i, out in enumerate((dq, dk, dv)):
            from_l, from_r = ret_rl[p, i], ret_rr[p, i]
            ua, ub = out[0, :UNIT, cols], out[0, UNIT:, cols]
            ua = high_from(split_l, ua, from_r)
            out[0, :UNIT, cols] = below(HEAD * (2 * sent_l + split_r), from_l, ua)
            ub = low_from(split_r, ub, from_l)
            out[0, UNIT:, cols] = below(
                2 * HEAD - HEAD * (2 * sent_r + split_l), ub, from_r
            )

    writes = [
        pltpu.make_async_copy(src, dst, out_sem.at[i])
        for i, (src, dst) in enumerate(((dq, dq_out), (dk, dk_out), (dv, dv_out)))
    ]
    for c in writes:
        c.start()

    for offset in range(1, nplane):
        source = lax.rem(spot + nplane - offset, nplane)
        shared(source, offset - 1, to_core).wait_recv()
        go(passed(source, offset))
    writes.append(pltpu.make_async_copy(final.at[core], final_out.at[core], out_sem.at[3]))
    writes[-1].start()
    for offset in range(nplane):
        passed(lax.rem(spot + nplane - offset, nplane), offset).wait_recv()
    writes.append(
        pltpu.make_async_copy(final.at[1 - core], final_out.at[1 - core], out_sem.at[4])
    )
    writes[-1].start()
    for c in sends + halo_l + halo_r:
        c.wait_send()
    for c in writes:
        c.wait()


def finish(nplane, dq, dk, dv, total, dq_out, dk_out, dv_out, wg_out, parts, final, wg, sem):
    flows = ((dq, dq_out), (dk, dk_out), (dv, dv_out))
    loads = [
        pltpu.make_async_copy(total.at[h], final.at[h], sem.at[h]) for h in range(2)
    ] + [
        pltpu.make_async_copy(src, parts.at[i], sem.at[2 + i]) for i, (src, _) in enumerate(flows)
    ]
    for c in loads:
        c.start()
    copies = []
    for h in range(2):
        loads[h].wait()
        for index in range(nplane):
            begin = (index * TILES) // nplane
            end = ((index + 1) * TILES) // nplane
            for t in range(begin, end):
                j, row = divmod(t * TILE, HALF)
                wg[h * HALF + row:h * HALF + row + TILE, j * 128:(j + 1) * 128] = final[
                    h, index, (t - begin) * TILE:(t - begin + 1) * TILE
                ].astype(F32)
        rows = pl.ds(h * HALF, HALF)
        copies.append(pltpu.make_async_copy(wg.at[rows], wg_out.at[rows], sem.at[5 + h]))
        copies[-1].start()
    for i, (_, dst) in enumerate(flows):
        loads[2 + i].wait()
        copies.append(pltpu.make_async_copy(parts.at[i], dst, sem.at[7 + i]))
        copies[-1].start()
    for c in copies:
        c.wait()


def shards(grid, queries, keys, values, outputs, out_grad, out_weight, slide_table):
    nx, nyl, nz, nyh, ncore = grid
    nplane = nx * nyl * nyh
    depth = -(-TILES // nplane) * TILE
    dma = pltpu.SemaphoreType.DMA
    part = (1, ROWS, FEATS)
    halo = (PAIRS, 4, UNIT, PAIR)
    back = (PAIRS, 3, UNIT, PAIR)
    parts = pl.pallas_call(
        functools.partial(kernel, grid),
        out_shape=[jax.ShapeDtypeStruct(part, BF16)] * 3
        + [jax.ShapeDtypeStruct((2, nplane, depth, 128), BF16)],
        in_specs=[pl.BlockSpec(memory_space=pltpu.SMEM)] + [pl.BlockSpec(memory_space=pl.ANY)] * 6,
        out_specs=[pl.BlockSpec(memory_space=pl.ANY)] * 4,
        scratch_shapes=[
            *[pltpu.VMEM(part, BF16)] * 4,
            pltpu.VMEM((1, ROWS, WIDTH), BF16),
            pltpu.VMEM((FEATS, WIDTH), BF16),
            dma((6,)),
            *[pltpu.VMEM(part, BF16)] * 3,
            pltpu.VMEM((2, nplane, depth, 128), BF16),
            dma((5,)),
            pltpu.VMEM((ROWS, FEATS), BF16),
            pltpu.VMEM(halo, BF16),
            pltpu.VMEM(halo, BF16),
            pltpu.VMEM(halo, BF16),
            pltpu.VMEM(halo, BF16),
            pltpu.VMEM((8, ROWS), F32),
            pltpu.VMEM((8, UNIT), F32),
            pltpu.VMEM((8, UNIT), F32),
            pltpu.VMEM((8, UNIT), F32),
            pltpu.VMEM((8, UNIT), F32),
            pltpu.VMEM(back, BF16),
            pltpu.VMEM(back, BF16),
            pltpu.VMEM(back, BF16),
            pltpu.VMEM(back, BF16),
            pltpu.VMEM((2, 4 * UNIT, 4 * UNIT), F32),
            pltpu.VMEM((4, 4 * UNIT, PAIR), BF16),
            pltpu.VMEM((4 * UNIT, 4 * UNIT), BF16),
            pltpu.VMEM((4 * UNIT, 4 * UNIT), BF16),
            pltpu.VMEM((PAIR, 4 * UNIT), F32),
            pltpu.VMEM((2, TILES * TILE, 128), BF16),
            pltpu.VMEM((TILES * TILE, 128), BF16),
            pltpu.VMEM((TILES * TILE, 128), BF16),
            pltpu.VMEM((nplane - 1, depth, 128), BF16),
            pltpu.VMEM((nz, depth, 128), BF16),
            dma((2, PAIRS)), dma((2, PAIRS)),
            dma((2,)), dma((2,)),
            dma((2, PAIRS)), dma((2, PAIRS)),
            dma, dma,
            dma((nplane - 1,)), dma((nplane - 1,)),
            dma((nz - 1,)), dma((nz - 1,)),
            dma((nplane - 1,)), dma((nplane - 1,)),
            dma((nplane,)), dma((nplane,)),
        ],
        compiler_params=pltpu.CompilerParams(
            collective_id=0, has_side_effects=True, vmem_limit_bytes=56 * 1024 * 1024
        ),
        name="attention_backward",
    )(slide_table, queries, keys, values, outputs, out_grad, out_weight)
    return pl.pallas_call(
        functools.partial(finish, nplane),
        out_shape=[jax.ShapeDtypeStruct(part, BF16)] * 3
        + [jax.ShapeDtypeStruct((FEATS, WIDTH), F32)],
        in_specs=[pl.BlockSpec(memory_space=pl.ANY)] * 4,
        out_specs=[pl.BlockSpec(memory_space=pl.ANY)] * 4,
        scratch_shapes=[
            pltpu.VMEM((3, *part), BF16),
            pltpu.VMEM((2, nplane, depth, 128), BF16),
            pltpu.VMEM((FEATS, WIDTH), F32),
            dma((10,)),
        ],
        compiler_params=pltpu.CompilerParams(vmem_limit_bytes=56 * 1024 * 1024),
        name="results",
    )(*parts)


def solution(mesh):
    rows = P("rep", "seq", None)
    return jax.shard_map(
        functools.partial(shards, GRID),
        mesh=mesh,
        in_specs=(rows, rows, rows, rows, rows, P(), P("rep", None)),
        out_specs=(rows, rows, rows, P()),
        check_vma=False,
    )
```

```python
import functools
import math

import jax
import jax.numpy as jnp
from jax import lax
from jax.experimental import pallas as pl
from jax.experimental.pallas import tpu as pltpu
from jax.sharding import PartitionSpec as P

HEAD = 64
UNIT = 128
PAIR = 128
ROWS = 256
FEATS = 384
WIDTH = 768
PAIRS = FEATS // PAIR
HALF = FEATS // 2
TILE = 16
TILES = HALF * WIDTH // (TILE * 128)
GRID = (4, 2, 8, 2, 2)
FAR = -1e30
MESH = pl.DeviceIdType.MESH
F32 = jnp.float32
BF16 = jnp.bfloat16


def nt(a, b):
    return lax.dot_general(a, b, (((1,), (1,)), ((), ())), preferred_element_type=F32)


def nn(a, b):
    return lax.dot_general(a, b, (((1,), (0,)), ((), ())), preferred_element_type=F32)


def roll_half(x):
    return jnp.concatenate([x[:, HEAD:], x[:, :HEAD]], axis=1)


def lanes(shape):
    return lax.broadcasted_iota(jnp.int32, shape, 1)


def below(limit, x, y):
    return jnp.where(lanes(x.shape) < limit, x, y)


def kernel(
    grid, tab, q_in, k_in, v_in, o_in, dy_in, w_in,
    dq_out, dk_out, dv_out, final_out,
    q, k, v, o, dy, w, load_sem, dq, dk, dv, final, out_sem,
    d_own, snd_l, snd_r, rcv_l, rcv_r, del_own, del_sl, del_sr, del_rl, del_rr,
    ret_sl, ret_sr, ret_rl, ret_rr, bias, win, p_buf, s_buf, q_turn,
    term, core_in, plane_out, plane_in, line,
    halo_send, halo_recv, del_send, del_recv, ret_send, ret_recv,
    core_send, core_recv, plane_send, plane_recv, line_send, line_recv,
    share_send, share_recv, swap_send, swap_recv,
):
    nx, nyl, nz, nyh, ncore = grid
    ny = nyl * nyh
    nplane = nx * ny
    depth = -(-TILES // nplane) * TILE
    nseq = nx * nyl * nz
    seq = lax.axis_index("seq")
    rep = lax.axis_index("rep")
    z = lax.rem(seq, nz)
    yl = lax.rem(seq // nz, nyl)
    x = seq // (nz * nyl)
    core = lax.rem(rep, ncore)
    yh = rep // ncore
    spot = x * ny + yh * nyl + yl
    left = lax.rem(seq + nseq - 1, nseq)
    right = lax.rem(seq + 1, nseq)
    to_left = (left, rep)
    to_right = (right, rep)
    to_core = (seq, yh * ncore + (ncore - 1 - core))

    def plane_peer(offset):
        other = lax.rem(spot + offset, nplane)
        oy = lax.rem(other, ny)
        device = ((other // ny) * nyl + lax.rem(oy, nyl)) * nz + z, (oy // nyl) * ncore + core
        return other, device

    def line_peer(offset):
        return ((seq - z) + lax.rem(z + offset, nz), rep)

    barrier = pltpu.get_barrier_semaphore()
    for peer in (to_left, to_right, to_core):
        pl.semaphore_signal(barrier, inc=1, device_id=peer, device_id_type=MESH)
    for offset in range(1, nplane):
        pl.semaphore_signal(barrier, inc=1, device_id=plane_peer(offset)[1], device_id_type=MESH)
    for offset in range(1, nz):
        pl.semaphore_signal(barrier, inc=1, device_id=line_peer(offset), device_id_type=MESH)

    loads = [
        pltpu.make_async_copy(src, dst, load_sem.at[i])
        for i, (src, dst) in enumerate(
            ((dy_in, dy), (w_in, w), (o_in, o), (q_in, q), (k_in, k), (v_in, v))
        )
    ]
    for c in loads:
        c.start()

    first = 2 * seq
    last_unit = 2 * nseq - 1

    def unit(step):
        return tab[0, jnp.clip(first + step, 0, last_unit)]

    flag = lambda cond: jnp.where(cond, 1, 0)
    l2, l1, a, b, r1, r2 = (unit(step) for step in (-2, -1, 0, 1, 2, 3))
    ab = flag(a == b)
    l21 = flag(l2 == l1)
    r12 = flag(r1 == r2)
    cross_l = flag(l1 == a) * flag(seq > 0)
    cross_r = flag(b == r1) * flag(seq < nseq - 1)
    split_r = cross_l * ab * l21
    split_l = cross_r * ab * r12
    recv_l = cross_l * ab * (1 - l21)
    sent_l = cross_l * (1 - ab)
    sent_r = cross_r * (1 - ab) * r12
    recv_r = cross_r * (1 - r12)

    low = lambda cond: HEAD * cond
    high = lambda cond: 2 * HEAD - HEAD * cond
    pick = lambda cond, yes, no: jnp.where(cond > 0, yes, no)

    def low_from(cond, x, y):
        return below(low(cond), roll_half(y), x)

    def high_from(cond, x, y):
        return below(high(cond), x, roll_half(y))

    def copy(src, dst, send, recv, peer):
        return pltpu.make_async_remote_copy(
            src_ref=src, dst_ref=dst, send_sem=send, recv_sem=recv,
            device_id=peer, device_id_type=MESH,
        )

    for c in loads[:3]:
        c.wait()
    d_own[...] = nt(dy[0], w[...]).astype(BF16)
    prod = d_own[...].astype(F32) * o[0].astype(F32)
    upper = prod.astype(BF16)
    lower = (prod - upper.astype(F32)).astype(BF16)
    chooser = (
        lax.broadcasted_iota(jnp.int32, (8, FEATS), 1) // HEAD
        == lax.broadcasted_iota(jnp.int32, (8, FEATS), 0)
    ).astype(F32).astype(BF16)
    del_own[...] = nt(chooser, upper) + nt(chooser, lower)

    for h in range(2 * PAIRS):
        even = h - h % 2
        da, db = del_own[h:h + 1, :UNIT], del_own[h:h + 1, UNIT:]
        if h % 2:
            db_even = del_own[even:even + 1, UNIT:]
            del_sl[h:h + 1] = below(UNIT * split_r, db_even, da)
            del_sr[h:h + 1] = db
        else:
            da_odd = del_own[h + 1:h + 2, :UNIT]
            del_sl[h:h + 1] = da
            del_sr[h:h + 1] = below(UNIT * split_l, da_odd, db)
    del_sl[6:8] = jnp.zeros((2, UNIT), F32)
    del_sr[6:8] = jnp.zeros((2, UNIT), F32)

    for c in loads[3:]:
        c.wait()
    sources = (q, k, v, None)
    for p in range(PAIRS):
        cols = slice(p * PAIR, (p + 1) * PAIR)
        for i, src in enumerate(sources):
            if src is None:
                ua, ub = d_own[:UNIT, cols], d_own[UNIT:, cols]
            else:
                ua, ub = src[0, :UNIT, cols], src[0, UNIT:, cols]
            snd_l[p, i] = high_from(split_r, ua, ub)
            snd_r[p, i] = low_from(split_l, ub, ua)

    for j in range(WIDTH // 128):
        block = lax.dot_general(
            o[0], dy[0, :, j * 128:(j + 1) * 128],
            (((0,), (0,)), ((), ())), preferred_element_type=F32,
        ).astype(BF16)
        for h in range(2):
            term[h, j * HALF:(j + 1) * HALF] = block[h * HALF:(h + 1) * HALF]

    pl.semaphore_wait(barrier, 3 + (nplane - 1) + (nz - 1))

    short = TILES // nplane * TILE

    def has_tail(index):
        return ((index + 1) * TILES) // nplane - (index * TILES) // nplane > TILES // nplane

    class Chunk:
        def __init__(self, index, make):
            self.either = ((make(short), jnp.logical_not(has_tail(index))),
                           (make(depth), has_tail(index)))
            if short == depth:
                self.either = ((make(depth), None),)

        def each(self, name):
            for c, cond in self.either:
                if cond is None:
                    getattr(c, name)()
                else:
                    pl.when(cond)(getattr(c, name))

        def start(self):
            self.each("start")

        def wait_recv(self):
            self.each("wait_recv")

        def wait_send(self):
            self.each("wait_send")

    sends = []

    def go(c):
        c.start()
        sends.append(c)
        return c

    deltas_in = [
        go(copy(del_sl, del_rr, del_send.at[0], del_recv.at[0], to_left)),
        go(copy(del_sr, del_rl, del_send.at[1], del_recv.at[1], to_right)),
    ]
    halo_l = [
        copy(snd_l.at[p], rcv_r.at[p], halo_send.at[0, p], halo_recv.at[0, p], to_left)
        for p in range(PAIRS)
    ]
    halo_r = [
        copy(snd_r.at[p], rcv_l.at[p], halo_send.at[1, p], halo_recv.at[1, p], to_right)
        for p in range(PAIRS)
    ]
    edge_l, edge_r = z == 0, z == nz - 1

    def forward(p, edges):
        for c, edge in ((halo_l[p], edge_l), (halo_r[p], edge_r)):
            if edges is None:
                c.start()
            else:
                pl.when(edge if edges else jnp.logical_not(edge))(c.start)

    core_copy = go(copy(term.at[1 - core], core_in, core_send, core_recv, to_core))
    forward(0, None)

    for par in range(2):
        mine_away = split_l if par else split_r
        theirs = split_r if par else split_l
        kinds = (
            pick(recv_l + theirs, a, -3),
            pick(sent_l + mine_away, -1, a),
            pick(sent_r + mine_away, -2, b),
            pick(recv_r + theirs, b, -4),
        )
        for i in range(4):
            for j in range(4):
                level = jnp.where(kinds[i] == kinds[j], F32(-2.0), F32(FAR))
                bias[par, i * UNIT:(i + 1) * UNIT, j * UNIT:(j + 1) * UNIT] = jnp.full(
                    (UNIT, UNIT), level, F32
                )

    core_copy.wait_recv()
    plane_out[...] = (term[core].astype(F32) + core_in[...].astype(F32)).astype(BF16)

    def chunk(index, rows):
        return pl.ds(pl.multiple_of((index * TILES) // nplane * TILE, TILE), rows)

    plane_in_copies = []
    for offset in range(1, nplane):
        other, peer = plane_peer(offset)

        def make(rows, other=other, peer=peer, i=offset - 1):
            return copy(
                plane_out.at[chunk(other, rows)], plane_in.at[i, pl.ds(0, rows)],
                plane_send.at[i], plane_recv.at[i], peer,
            )

        go(Chunk(other, make))
        plane_in_copies.append(Chunk(spot, make))

    forward(1, False)
    forward(2, False)

    scale = 0.125 * math.log2(math.e)

    def arrive(p):
        halo_l[p].wait_recv()
        halo_r[p].wait_recv()

    def attend(p):
        cols = slice(p * PAIR, (p + 1) * PAIR)
        for i, src in enumerate(sources):
            win[i, :UNIT] = low_from(split_l, rcv_l[p, i], rcv_r[p, i])
            win[i, UNIT:3 * UNIT] = d_own[:, cols] if src is None else src[0, :, cols]
            win[i, 3 * UNIT:] = high_from(split_r, rcv_r[p, i], rcv_l[p, i])
        key_turn = win[1].T
        d_keys, d_values = [], []
        for par in range(2):
            h = 2 * p + par
            own = del_own[h:h + 1]
            if par:
                d0 = del_rl[h:h + 1]
                d3 = below(UNIT * split_r, del_rl[h - 1:h], del_rr[h:h + 1])
                zero = jnp.zeros_like(win[1])
                key_one = below(HEAD, zero, win[1])
                value_one = below(HEAD, zero, win[2])
            else:
                d0 = below(UNIT * split_l, del_rr[h + 1:h + 2], del_rl[h:h + 1])
                d3 = del_rr[h:h + 1]
                zero = jnp.zeros_like(win[1])
                key_one = below(HEAD, win[1], zero)
                value_one = below(HEAD, win[2], zero)
            delta_halves = (
                jnp.concatenate([d0, own[:, :UNIT]], axis=1),
                jnp.concatenate([own[:, UNIT:], d3], axis=1),
            )
            for half in range(2):
                part = slice(half * 256, half * 256 + 256)
                scores = nt(key_one, win[0, part])
                expo = jnp.exp2(scores * scale + bias[par, :, part])
                totals = jnp.sum(expo, axis=0, keepdims=True)
                probs = expo * (1.0 / totals)
                d_prob = nt(value_one, win[3, part])
                d_score = (probs * (d_prob - delta_halves[half])).astype(BF16)
                p_buf[:, part] = probs.astype(BF16)
                s_buf[:, part] = d_score
                q_turn[par * HEAD:(par + 1) * HEAD, part] = nn(
                    key_turn[par * HEAD:(par + 1) * HEAD], d_score
                )
            d_values.append(nn(p_buf[...], win[3]))
            d_keys.append(nn(s_buf[...], win[0]))
        grads = (
            (dq, 0.125 * q_turn[...].T),
            (dk, 0.125 * below(HEAD, d_keys[0], d_keys[1])),
            (dv, below(HEAD, d_values[0], d_values[1])),
        )
        for i, (out, grad) in enumerate(grads):
            grad = grad.astype(BF16)
            out[0, :, cols] = grad[UNIT:3 * UNIT]
            before, after = grad[:UNIT], grad[3 * UNIT:]
            ret_sl[p, i] = low_from(split_r, before, after)
            ret_sr[p, i] = high_from(split_l, after, before)

    returns = []

    def give_back(p):
        returns.append([
            go(copy(ret_sl.at[p], ret_rr.at[p], ret_send.at[0, p], ret_recv.at[0, p], to_left)),
            go(copy(ret_sr.at[p], ret_rl.at[p], ret_send.at[1, p], ret_recv.at[1, p], to_right)),
        ])

    for c in deltas_in:
        c.wait_recv()
    arrive(0)
    forward(1, True)
    forward(2, True)
    attend(0)

    for c in plane_in_copies:
        c.wait_recv()
    total = plane_out[chunk(spot, depth)].astype(F32)
    for offset in range(1, nplane):
        total = total + plane_in[offset - 1].astype(F32)
    line[z] = total.astype(BF16)
    line_copies = []
    for offset in range(1, nz):
        line_copies.append(go(Chunk(spot, lambda rows, offset=offset: copy(
            line.at[z, pl.ds(0, rows)], line.at[z, pl.ds(0, rows)],
            line_send.at[offset - 1], line_recv.at[offset - 1], line_peer(offset),
        ))))

    give_back(0)
    arrive(1)
    attend(1)
    give_back(1)

    for c in line_copies:
        c.wait_recv()
    total = line[0].astype(F32)
    for index in range(1, nz):
        total = total + line[index].astype(F32)
    norm = 1.0 / math.sqrt(nseq * ROWS * nyh * ncore)
    final[core, spot] = (total * norm).astype(BF16)

    def passed(index, i):
        def make(rows):
            part = final.at[core, index, pl.ds(0, rows)]
            return copy(part, part, swap_send.at[i], swap_recv.at[i], to_core)
        return Chunk(index, make)

    def shared(index, i, peer):
        def make(rows):
            part = final.at[core, index, pl.ds(0, rows)]
            return copy(part, part, share_send.at[i], share_recv.at[i], peer)
        return Chunk(index, make)

    for offset in range(1, nplane):
        go(shared(spot, offset - 1, plane_peer(offset)[1]))
    go(passed(spot, 0))

    arrive(2)
    attend(2)
    give_back(2)

    for p in range(PAIRS):
        for c in returns[p]:
            c.wait_recv()
        cols = slice(p * PAIR, (p + 1) * PAIR)
        for i, out in enumerate((dq, dk, dv)):
            from_l, from_r = ret_rl[p, i], ret_rr[p, i]
            ua, ub = out[0, :UNIT, cols], out[0, UNIT:, cols]
            ua = high_from(split_l, ua, from_r)
            out[0, :UNIT, cols] = below(HEAD * (2 * sent_l + split_r), from_l, ua)
            ub = low_from(split_r, ub, from_l)
            out[0, UNIT:, cols] = below(
                2 * HEAD - HEAD * (2 * sent_r + split_l), ub, from_r
            )

    writes = [
        pltpu.make_async_copy(src, dst, out_sem.at[i])
        for i, (src, dst) in enumerate(((dq, dq_out), (dk, dk_out), (dv, dv_out)))
    ]
    for c in writes:
        c.start()

    for offset in range(1, nplane):
        source = lax.rem(spot + nplane - offset, nplane)
        shared(source, offset - 1, to_core).wait_recv()
        go(passed(source, offset))
    writes.append(pltpu.make_async_copy(final.at[core], final_out.at[core], out_sem.at[3]))
    writes[-1].start()
    for offset in range(nplane):
        passed(lax.rem(spot + nplane - offset, nplane), offset).wait_recv()
    writes.append(
        pltpu.make_async_copy(final.at[1 - core], final_out.at[1 - core], out_sem.at[4])
    )
    writes[-1].start()
    for c in sends + halo_l + halo_r:
        c.wait_send()
    for c in writes:
        c.wait()


def finish(nplane, dq, dk, dv, total, dq_out, dk_out, dv_out, wg_out, parts, final, wg, sem):
    flows = ((dq, dq_out), (dk, dk_out), (dv, dv_out))
    loads = [
        pltpu.make_async_copy(total.at[h], final.at[h], sem.at[h]) for h in range(2)
    ] + [
        pltpu.make_async_copy(src, parts.at[i], sem.at[2 + i]) for i, (src, _) in enumerate(flows)
    ]
    for c in loads:
        c.start()
    copies = []
    for h in range(2):
        loads[h].wait()
        for index in range(nplane):
            begin = (index * TILES) // nplane
            end = ((index + 1) * TILES) // nplane
            for t in range(begin, end):
                j, row = divmod(t * TILE, HALF)
                wg[h * HALF + row:h * HALF + row + TILE, j * 128:(j + 1) * 128] = final[
                    h, index, (t - begin) * TILE:(t - begin + 1) * TILE
                ].astype(F32)
        rows = pl.ds(h * HALF, HALF)
        copies.append(pltpu.make_async_copy(wg.at[rows], wg_out.at[rows], sem.at[5 + h]))
        copies[-1].start()
    for i, (_, dst) in enumerate(flows):
        loads[2 + i].wait()
        copies.append(pltpu.make_async_copy(parts.at[i], dst, sem.at[7 + i]))
        copies[-1].start()
    for c in copies:
        c.wait()


def shards(grid, queries, keys, values, outputs, out_grad, out_weight, slide_table):
    nx, nyl, nz, nyh, ncore = grid
    nplane = nx * nyl * nyh
    depth = -(-TILES // nplane) * TILE
    dma = pltpu.SemaphoreType.DMA
    part = (1, ROWS, FEATS)
    halo = (PAIRS, 4, UNIT, PAIR)
    back = (PAIRS, 3, UNIT, PAIR)
    parts = pl.pallas_call(
        functools.partial(kernel, grid),
        out_shape=[jax.ShapeDtypeStruct(part, BF16)] * 3
        + [jax.ShapeDtypeStruct((2, nplane, depth, 128), BF16)],
        in_specs=[pl.BlockSpec(memory_space=pltpu.SMEM)] + [pl.BlockSpec(memory_space=pl.ANY)] * 6,
        out_specs=[pl.BlockSpec(memory_space=pl.ANY)] * 4,
        scratch_shapes=[
            *[pltpu.VMEM(part, BF16)] * 4,
            pltpu.VMEM((1, ROWS, WIDTH), BF16),
            pltpu.VMEM((FEATS, WIDTH), BF16),
            dma((6,)),
            *[pltpu.VMEM(part, BF16)] * 3,
            pltpu.VMEM((2, nplane, depth, 128), BF16),
            dma((5,)),
            pltpu.VMEM((ROWS, FEATS), BF16),
            pltpu.VMEM(halo, BF16),
            pltpu.VMEM(halo, BF16),
            pltpu.VMEM(halo, BF16),
            pltpu.VMEM(halo, BF16),
            pltpu.VMEM((8, ROWS), F32),
            pltpu.VMEM((8, UNIT), F32),
            pltpu.VMEM((8, UNIT), F32),
            pltpu.VMEM((8, UNIT), F32),
            pltpu.VMEM((8, UNIT), F32),
            pltpu.VMEM(back, BF16),
            pltpu.VMEM(back, BF16),
            pltpu.VMEM(back, BF16),
            pltpu.VMEM(back, BF16),
            pltpu.VMEM((2, 4 * UNIT, 4 * UNIT), F32),
            pltpu.VMEM((4, 4 * UNIT, PAIR), BF16),
            pltpu.VMEM((4 * UNIT, 4 * UNIT), BF16),
            pltpu.VMEM((4 * UNIT, 4 * UNIT), BF16),
            pltpu.VMEM((PAIR, 4 * UNIT), F32),
            pltpu.VMEM((2, TILES * TILE, 128), BF16),
            pltpu.VMEM((TILES * TILE, 128), BF16),
            pltpu.VMEM((TILES * TILE, 128), BF16),
            pltpu.VMEM((nplane - 1, depth, 128), BF16),
            pltpu.VMEM((nz, depth, 128), BF16),
            dma((2, PAIRS)), dma((2, PAIRS)),
            dma((2,)), dma((2,)),
            dma((2, PAIRS)), dma((2, PAIRS)),
            dma, dma,
            dma((nplane - 1,)), dma((nplane - 1,)),
            dma((nz - 1,)), dma((nz - 1,)),
            dma((nplane - 1,)), dma((nplane - 1,)),
            dma((nplane,)), dma((nplane,)),
        ],
        compiler_params=pltpu.CompilerParams(
            collective_id=0, has_side_effects=True, vmem_limit_bytes=56 * 1024 * 1024
        ),
        name="attention_backward",
    )(slide_table, queries, keys, values, outputs, out_grad, out_weight)
    return pl.pallas_call(
        functools.partial(finish, nplane),
        out_shape=[jax.ShapeDtypeStruct(part, BF16)] * 3
        + [jax.ShapeDtypeStruct((FEATS, WIDTH), F32)],
        in_specs=[pl.BlockSpec(memory_space=pl.ANY)] * 4,
        out_specs=[pl.BlockSpec(memory_space=pl.ANY)] * 4,
        scratch_shapes=[
            pltpu.VMEM((3, *part), BF16),
            pltpu.VMEM((2, nplane, depth, 128), BF16),
            pltpu.VMEM((FEATS, WIDTH), F32),
            dma((10,)),
        ],
        compiler_params=pltpu.CompilerParams(vmem_limit_bytes=56 * 1024 * 1024),
        name="results",
    )(*parts)


def solution(mesh):
    rows = P("rep", "seq", None)
    return jax.shard_map(
        functools.partial(shards, GRID),
        mesh=mesh,
        in_specs=(rows, rows, rows, rows, rows, P(), P("rep", None)),
        out_specs=(rows, rows, rows, P()),
        check_vma=False,
    )
```
